256 devices in a mesh: rows: 64 (over y, z, core), groups: 4 (over x).
Axes of the slice: x: 4, y: 4, z: 8, core: 2. Of those that a mesh axis runs over, the one named last changes fastest.
Arguments:
- snapshots: bfloat16 [131072, 1024], P('rows', 'groups'), may hold values from -6 to 6
- mass_diag: float32 [131072], P('rows'), may hold values from 0.5 to 2
- lower_coupling: float32 [64, 128, 128], P('rows'), may hold values from -0.5 to 0.5
- upper_coupling: float32 [64, 128, 128], P('rows'), may hold values from -0.5 to 0.5
- band_offsets: int32 [64, 2], P('rows'), may hold values from 1 to 2
- start_basis: float32 [1024, 512], replicated, may hold values from -6 to 6
Outputs:
- modes: float32 [131072, 512], P('rows', 'groups')
The draws below stay inside these ranges and needn't reach their ends.
All inputs are finite; a program needn't handle non-finite values.
Results may differ from the reference program's by a relative error of at most 0.0042.
Values may be sent and summed in bfloat16 or wider, within the bound.
No kernel may reach another device: no remote copies, remote signals or barrier semaphores. Data moves between devices by JAX's collectives and lax.ppermute only.
A program may use at most 128 MiB of HBM per device.

```python
import math
import jax
import jax.numpy as jnp
from jax import lax

RB = 2048
NSNAP = 1024
MODES = 512
H = 128
ITERS = 3
NBLK = 64
NROWS = 131072


def with_ends(values, stream_key, low, top_value):
    longest = values.shape.index(max(values.shape))
    spots = []
    for shift in (0, 1):
        where = [jax.random.randint(jax.random.fold_in(stream_key, axis), (), 0, length) for axis, length in enumerate(values.shape)]
        where[longest] = (where[longest] + shift) % values.shape[longest]
        spots.append(tuple(where))
    return values.at[spots[0]].set(low).at[spots[1]].set(top_value)


def steps_of(own_key, dims, pieces, smallest, largest):
    def one(position, parts):
        steps = jax.random.uniform(jax.random.fold_in(jax.random.fold_in(own_key, 6), position), (parts,), jnp.float32, smallest / len(pieces), largest / len(pieces))
        return jnp.repeat(jnp.exp(steps), dims[position] // parts).reshape((-1,) + (1,) * (len(dims) - position - 1))

    factor_of = one(*pieces[0])
    for cut in pieces[1:]:
        factor_of = factor_of * one(*cut)
    return factor_of


def normal_values(stream_key, dims, width, limit, pieces=(), held_as=jnp.bfloat16):
    entries = jax.random.normal(stream_key, dims, jnp.float32) * width
    if len(pieces) > 0:
        entries = steps_of(stream_key, dims, pieces, -0.22, 0.18) * entries
    return jnp.clip(entries, min=-limit, max=limit).astype(held_as)


def setup_inputs(seed: int = 0) -> dict:
    splits = jax.random.split(jax.random.key(seed), 7)
    return {
        "snapshots": normal_values(splits[0], (NROWS, NSNAP), 1.0, 6.0, ((0, 64), (1, 4))),
        "mass_diag": jnp.clip(jnp.exp(math.log(2.0) - 1.3862944 * jax.random.uniform(splits[1], (NROWS,), jnp.float32) ** steps_of(splits[1], (NROWS,), ((0, 64),), -0.2, 0.2)), 0.5, 2.0),
        "lower_coupling": normal_values(splits[2], (NBLK, H, H), H ** -0.5, 0.5, ((0, 64),), jnp.float32),
        "upper_coupling": normal_values(splits[3], (NBLK, H, H), H ** -0.5, 0.5, ((0, 64),), jnp.float32),
        "band_offsets": with_ends(jax.random.randint(splits[4], (NBLK, 2), 1, 3), jax.random.fold_in(splits[4], 1), 1, 2).astype(jnp.int32),
        "start_basis": normal_values(splits[5], (NSNAP, MODES), 1.0, 6.0, (), jnp.float32),
    }


def orthonormal(image):
    correlation = jnp.dot(image.T.astype(jnp.float32), image.astype(jnp.float32), precision=lax.Precision.HIGHEST, preferred_element_type=jnp.float32)
    lower = jnp.linalg.cholesky(correlation)
    return lax.linalg.triangular_solve(lower, image, left_side=False, lower=True, transpose_a=True)

def reference(snapshots, mass_diag, lower_coupling, upper_coupling, band_offsets, start_basis):
    blocks = snapshots.reshape(NBLK, RB, NSNAP)
    bottom = blocks[:, RB - H:, :].astype(jnp.float32)
    top = blocks[:, :H, :].astype(jnp.float32)
    block_ids = jnp.arange(NBLK, dtype=jnp.int32)
    lower_ids = block_ids - band_offsets[:, 0]
    upper_ids = block_ids + band_offsets[:, 1]
    lower_ok = (lower_ids >= 0).astype(jnp.float32)[:, None, None]
    upper_ok = (upper_ids < NBLK).astype(jnp.float32)[:, None, None]
    lower_rims = bottom[jnp.clip(lower_ids, 0, NBLK - 1)] * lower_ok
    upper_rims = top[jnp.clip(upper_ids, 0, NBLK - 1)] * upper_ok
    lower_terms = jnp.einsum('ihk,iks->ihs', lower_coupling, lower_rims, precision=lax.Precision.HIGHEST)
    upper_terms = jnp.einsum('ihk,iks->ihs', upper_coupling, upper_rims, precision=lax.Precision.HIGHEST)
    weighted = mass_diag.reshape(NBLK, RB, 1) * blocks.astype(jnp.float32)
    weighted = weighted.at[:, :H, :].add(lower_terms)
    weighted = weighted.at[:, RB - H:, :].add(upper_terms)
    weighted = weighted.reshape(NROWS, NSNAP).astype(jnp.bfloat16)
    gram = jnp.dot(weighted.T.astype(jnp.float32), weighted.astype(jnp.float32), preferred_element_type=jnp.float32) / NROWS
    basis = start_basis
    for turn_index in range(ITERS):
        image = jnp.dot(gram.astype(jnp.float32), basis.astype(jnp.float32), precision=lax.Precision.HIGHEST, preferred_element_type=jnp.float32)
        basis = orthonormal(image)
    basis_low = basis.astype(jnp.bfloat16)
    return jnp.dot(weighted.astype(jnp.float32), basis_low.astype(jnp.float32), preferred_element_type=jnp.float32)
```

```python
import functools

import jax
import jax.numpy as jnp
from jax import lax
from jax.experimental import pallas as pl
from jax.experimental.pallas import tpu as pltpu
from jax.sharding import PartitionSpec as P

F32 = jnp.float32
BF16 = jnp.bfloat16
BLOCK = 128
PANEL = 8


def split(value):
    high = value.astype(BF16)
    return high, (value - high.astype(F32)).astype(BF16)


def dot3(left, right, dims):
    lh, ll = left
    rh, rl = right
    one = lambda a, b: lax.dot_general(a, b, (dims, ((), ())), preferred_element_type=F32)
    return one(lh, rh) + (one(lh, rl) + one(ll, rh))


def factor_block(m):
    n = m.shape[0]
    lanes = lax.broadcasted_iota(jnp.int32, (1, n), 1)
    subs = lax.broadcasted_iota(jnp.int32, (PANEL, n), 0)
    done = []
    for k in range(0, n, PANEL):
        top = m[:PANEL]
        rest = m[PANEL:]
        rows = [jnp.broadcast_to(top[a : a + 1], (PANEL, n)) for a in range(PANEL)]
        e = {}
        for a in range(PANEL):
            for j in range(a, PANEL):
                e[a, j] = jnp.broadcast_to(rows[a][:, k + j : k + j + 1], (PANEL, n))
        rows = [
            jnp.where(lanes == k + a, 1.0, jnp.where((lanes >= k) & (lanes < k + PANEL), 0.0, rows[a]))
            for a in range(PANEL)
        ]
        inv = []
        low = {}
        for a in range(PANEL):
            inv.append(1.0 / e[a, a])
            for b in range(a + 1, PANEL):
                low[b, a] = e[a, b] * inv[a]
            for b in range(a + 1, PANEL):
                for j in range(b, PANEL):
                    e[b, j] = e[b, j] - low[b, a] * e[a, j]
                rows[b] = rows[b] - low[b, a] * rows[a]
        out = rows[0] * lax.rsqrt(e[0, 0])
        for a in range(1, PANEL):
            out = jnp.where(subs == a, rows[a] * lax.rsqrt(e[a, a]), out)
        done.append(out)
        if k + PANEL == n:
            break
        q = [rows[a] * inv[a] for a in range(PANEL)]
        for a in reversed(range(PANEL)):
            for b in range(a + 1, PANEL):
                q[a] = q[a] - low[b, a] * q[b]
        height = n - k - PANEL
        inside = (lanes >= k) & (lanes < k + PANEL)
        acc = jnp.where(inside, 0.0, rest)
        for j in range(PANEL):
            col = jnp.broadcast_to(rest[:, k + j : k + j + 1], (height, n))
            acc = acc - col * q[j][:1]
        m = acc
    return jnp.concatenate(done, axis=0)


def inverse_factor(m_ref):
    n = m_ref.shape[0]
    cols = lax.broadcasted_iota(jnp.int32, (1, n), 1)
    rows = lax.broadcasted_iota(jnp.int32, (n, 1), 0)

    def step(j, carry):
        lo = pl.multiple_of(j * BLOCK, BLOCK)
        w = factor_block(m_ref[pl.ds(lo, BLOCK), pl.ds(lo, BLOCK)])
        r = lax.broadcasted_iota(jnp.int32, (BLOCK, BLOCK), 0)
        c = lax.broadcasted_iota(jnp.int32, (BLOCK, BLOCK), 1)
        w = jnp.where(r >= c, w, 0.0)
        ws = split(w)
        panel = m_ref[pl.ds(lo, BLOCK), :]
        z = dot3(ws, split(panel), ((1,), (0,)))
        m_ref[pl.ds(lo, BLOCK), :] = z
        m_ref[pl.ds(lo, BLOCK), pl.ds(lo, BLOCK)] = w
        z = m_ref[pl.ds(lo, BLOCK), :]
        y = jnp.where(cols >= lo + BLOCK, z, 0.0)
        below = rows >= lo + BLOCK
        inside = (cols >= lo) & (cols < lo + BLOCK)
        m = m_ref[...]
        m = jnp.where(below & inside, 0.0, m)
        m_ref[...] = m - dot3(split(y), split(z), ((0,), (0,)))
        return carry

    lax.fori_loop(0, n // BLOCK, step, 0)


def assemble(core, mine_ref, other_ref, gram_ref, gh_ref, gl_ref):
    n = gram_ref.shape[0]
    groups = 4
    size = n // groups
    lanes = size // 2

    def block(group, which, ref, half):
        lo = (group * 3 + which) * size
        return ref[lo : lo + size, :]

    at = pl.multiple_of(core * lanes, lanes)
    off = pl.multiple_of((1 - core) * lanes, lanes)
    for group in range(groups):
        col = group * size
        for which in range(3):
            row = ((group + which) % groups) * size
            for ref, shift in ((mine_ref, at), (other_ref, off)):
                gram_ref[row : row + size, pl.ds(pl.multiple_of(col + shift, lanes), lanes)] = block(group, which, ref, 0)
    for group in range(groups):
        a, b = group * size, ((group + 1) % groups) * size
        gram_ref[a : a + size, b : b + size] = gram_ref[b : b + size, a : a + size].T
    for group in range(groups // 2):
        a, b = group * size, (group + 2) * size
        both = gram_ref[b : b + size, a : a + size] + gram_ref[a : a + size, b : b + size].T
        gram_ref[b : b + size, a : a + size] = both
        gram_ref[a : a + size, b : b + size] = both.T
    gh, gl = split(gram_ref[...])
    gh_ref[...] = gh
    gl_ref[...] = gl


def iterate_kernel(iters, where_ref, mine_ref, other_ref, s_ref, out_ref, gram_ref, gh_ref, gl_ref, image_ref, basis_ref, m_ref):
    assemble(where_ref[1], mine_ref, other_ref, gram_ref, gh_ref, gl_ref)
    basis_ref[...] = s_ref[...]
    n = m_ref.shape[0]

    def turn_index(i, carry):
        bs = split(basis_ref[...])
        image_ref[...] = dot3((gh_ref[...], gl_ref[...]), bs, ((1,), (0,)))
        parts = split(image_ref[...])
        m_ref[...] = dot3(parts, parts, ((0,), (0,)))
        inverse_factor(m_ref)
        r = lax.broadcasted_iota(jnp.int32, (n, n), 0)
        c = lax.broadcasted_iota(jnp.int32, (n, n), 1)
        w = jnp.where(r >= c, m_ref[...], 0.0)
        basis_ref[...] = dot3(split(image_ref[...]), split(w), ((1,), (1,)))
        return carry

    lax.fori_loop(0, iters, turn_index, 0)
    groups = 4
    size = basis_ref.shape[0] // groups
    cols = n // groups
    group = where_ref[0]
    for q in range(groups):
        row = pl.multiple_of(lax.rem(group + q, groups) * size, size)
        part = basis_ref[pl.ds(row, size), pl.ds(pl.multiple_of(group * cols, cols), cols)]
        out_ref[q * size : (q + 1) * size, :] = part.astype(BF16)


def iterate(where, mine, other, start, iters):
    n, k = start.shape
    return pl.pallas_call(
        functools.partial(iterate_kernel, iters),
        out_shape=jax.ShapeDtypeStruct((n, k // 4), BF16),
        in_specs=[pl.BlockSpec(memory_space=pltpu.SMEM)] + [pl.BlockSpec(memory_space=pltpu.VMEM)] * 3,
        out_specs=pl.BlockSpec(memory_space=pltpu.VMEM),
        scratch_shapes=[
            pltpu.VMEM((n, n), F32),
            pltpu.VMEM((n, n), BF16),
            pltpu.VMEM((n, n), BF16),
            pltpu.VMEM((n, k), F32),
            pltpu.VMEM((n, k), F32),
            pltpu.VMEM((k, k), F32),
        ],
        compiler_params=pltpu.CompilerParams(vmem_limit_bytes=52 * 2**20),
        cost_estimate=pl.CostEstimate(flops=60 * 10**9, bytes_accessed=8 * 2**20, transcendentals=0),
    )(where, mine, other, start)


def modes_kernel(h, *refs):
    *pairs, basis_ref, out_ref = refs
    inner, rims = pairs[:4], pairs[4:]
    rows = out_ref.shape[0]
    size = basis_ref.shape[0] // 4

    def project(refs, lo, hi):
        total = None
        for q, ref in enumerate(refs):
            term = jnp.dot(ref[lo:hi, :], basis_ref[q * size : (q + 1) * size, :], preferred_element_type=F32)
            total = term if total is None else total + term
        return total

    out_ref[:h, :] = project(rims, 0, h)
    out_ref[rows - h :, :] = project(rims, h, 2 * h)
    out_ref[h : rows - h, :] = project(inner, 0, rows - 2 * h)


def modes(own, following, across, behind, basis, rows, h):
    parts = [[p[i] for p in (own, following, across, behind)] for i in (0, 1)]
    return pl.pallas_call(
        functools.partial(modes_kernel, h),
        out_shape=jax.ShapeDtypeStruct((rows, basis.shape[1]), F32),
        in_specs=[pl.BlockSpec(memory_space=pltpu.VMEM)] * 9,
        out_specs=pl.BlockSpec(memory_space=pltpu.VMEM),
        compiler_params=pltpu.CompilerParams(vmem_limit_bytes=40 * 2**20),
    )(*parts[0], *parts[1], basis)


ITERS = 3
ROWS = ("y", "z", "core")


def shift_rows(value, by):
    blocks = lax.axis_size("y") * lax.axis_size("z") * lax.axis_size("core")
    pairs = [(i, i + by) for i in range(blocks) if 0 <= i + by < blocks]
    return lax.ppermute(value, ROWS, pairs)


def turn(value, axis, by):
    size = lax.axis_size(axis)
    return lax.ppermute(value, axis, [(i, (i + by) % size) for i in range(size)])


def spread(value, axis):
    size = 1
    for name in axis if isinstance(axis, tuple) else (axis,):
        size *= lax.axis_size(name)
    copies = jnp.broadcast_to(value[None], (size,) + value.shape).reshape((size * value.shape[0],) + value.shape[1:])
    return lax.all_to_all(copies, axis, 0, 0, tiled=True)


def cross(left, right):
    return lax.dot_general(left, right, (((0,), (0,)), ((), ())), preferred_element_type=F32)


def rim(snaps, mass, coupling, near, far, offset):
    other = jnp.where(offset == 1, near, far).astype(F32)
    terms = jnp.dot(coupling, other, precision=lax.Precision.HIGHEST, preferred_element_type=F32)
    return (mass[:, None] * snaps.astype(F32) + terms).astype(BF16)


def shards(snapshots, mass_diag, lower_coupling, upper_coupling, band_offsets, start_basis):
    block_rows, width = snapshots.shape
    h = lower_coupling.shape[1]
    total_rows = block_rows * lax.axis_size(ROWS)
    group = lax.axis_index("x")
    core = lax.axis_index("core")

    top, bottom = snapshots[:h], snapshots[block_rows - h :]
    below = [shift_rows(bottom, 1), shift_rows(bottom, 2)]
    above = [shift_rows(top, -1), shift_rows(top, -2)]
    inner = (mass_diag[h : block_rows - h, None] * snapshots[h : block_rows - h].astype(F32)).astype(BF16)
    rims = jnp.concatenate(
        [
            rim(top, mass_diag[:h], lower_coupling[0], below[0], below[1], band_offsets[0, 0]),
            rim(bottom, mass_diag[block_rows - h :], upper_coupling[0], above[0], above[1], band_offsets[0, 1]),
        ],
        axis=0,
    )

    own, following, facing = [], [], []
    for piece in (inner, rims):
        part = piece.shape[0] // 2
        first = group < 2
        own_half = lax.dynamic_slice_in_dim(piece, jnp.where(first, 0, part), part, 0)
        send_half = lax.dynamic_slice_in_dim(piece, jnp.where(first, part, 0), part, 0)
        own.append(piece)
        following.append(turn(piece, "x", -1))
        facing.append((turn(send_half, "x", 2), own_half))
    blocks = [
        sum(cross(p, p) for p in own),
        sum(cross(f, p) for f, p in zip(following, own)),
        sum(cross(f, p) for f, p in facing),
    ]
    partial = jnp.concatenate(blocks, axis=0)
    lanes = width // 2
    keep = lax.dynamic_slice_in_dim(partial, core * lanes, lanes, 1)
    give = lax.dynamic_slice_in_dim(partial, (1 - core) * lanes, lanes, 1)
    chip = keep + turn(give, "core", 1)
    sources = lax.axis_size(("y", "z"))
    pieces = lax.all_to_all(chip, ("y", "z"), 0, 0, tiled=True)
    share = pieces.reshape((sources, -1, lanes)).sum(0) / total_rows
    halves = spread(spread(share, "z"), ("x", "y"))
    other_halves = turn(halves, "core", 1)

    own, following, halves, other_halves = lax.optimization_barrier((own, following, halves, other_halves))
    behind = [turn(p, "x", 1) for p in own]
    across = [turn(p, "x", 2) for p in own]
    where = jnp.stack([group, core]).astype(jnp.int32)
    basis = iterate(where, halves, other_halves, start_basis, ITERS)
    return modes(own, following, across, behind, basis, block_rows, h)


def solution(mesh):
    fine = jax.sharding.Mesh(mesh.devices.reshape(4, 8, 2, 4), ("y", "z", "core", "x"))
    placed = (
        P(ROWS, "x"),
        P(ROWS),
        P(ROWS, None, None),
        P(ROWS, None, None),
        P(ROWS, None),
        P(),
    )
    return jax.shard_map(shards, mesh=fine, in_specs=placed, out_specs=P(ROWS, "x"), check_vma=False)
```

```python
import functools

import jax
import jax.numpy as jnp
from jax import lax
from jax.experimental import pallas as pl
from jax.experimental.pallas import tpu as pltpu
from jax.sharding import PartitionSpec as P

F32 = jnp.float32
BF16 = jnp.bfloat16
GROUPS = 4
BLOCK = 128
TILE = 8
WINDOW = 16
ROW_COL = ((1,), (0,))
ROW_ROW = ((1,), (1,))


def split(value):
    high = value.astype(BF16)
    return high, (value - high.astype(F32)).astype(BF16)


def dot3(left, right, dims):
    one = lambda a, b: lax.dot_general(a, b, (dims, ((), ())), preferred_element_type=F32)
    return one(left[0], right[0]) + (one(left[0], right[1]) + one(left[1], right[0]))


def row(tile, index):
    return jnp.broadcast_to(tile[index : index + 1], tile.shape)


def column(tile, index):
    return jnp.broadcast_to(tile[:, index : index + 1], tile.shape)


def total(terms):
    while len(terms) > 1:
        terms = [sum(terms[i : i + 2][1:], terms[i]) for i in range(0, len(terms), 2)]
    return terms[0]


def inverse_block(m, beside):
    n = m.shape[0]
    tiles = WINDOW // TILE
    lanes = lax.broadcasted_iota(jnp.int32, (1, n), 1)
    subs = lax.broadcasted_iota(jnp.int32, (TILE, n), 0)
    done = []
    near = [m[s * TILE : (s + 1) * TILE] for s in range(tiles)]
    rest = m[WINDOW:]
    for k in range(0, n, WINDOW):
        for _ in range(-(-len(beside) * WINDOW // (n - k))):
            beside.pop(0)()
        inside = (lanes >= k) & (lanes < k + WINDOW)
        cols = [[column(near[s], k + j) for j in range((s + 1) * TILE)] for s in range(tiles)]
        rows = [
            jnp.where(inside, jnp.where(lanes == subs + (k + s * TILE), 1.0, 0.0), near[s]) for s in range(tiles)
        ]
        entry, pivot_row, inverse = {}, {}, {}
        for a in range(0, WINDOW, 2):
            b, t = a + 1, a // TILE
            for p in (a, b):
                entry[p] = {j: row(cols[j // TILE][p], j % TILE) for j in range(p, WINDOW)}
                pivot_row[p] = row(rows[t], p % TILE)
            aa, ab, bb = entry[a][a], entry[a][b], entry[b][b]
            inverse[a] = 1.0 / (aa * bb - ab * ab)
            for s in range(t, tiles):
                if s == t and b % TILE == TILE - 1:
                    continue
                to_a = cols[s][a] * bb - cols[s][b] * ab
                to_b = cols[s][b] * aa - cols[s][a] * ab
                if s == t:
                    later = subs > b % TILE
                    to_a, to_b = jnp.where(later, to_a, 0.0), jnp.where(later, to_b, 0.0)
                for j in range(b + 1, (s + 1) * TILE):
                    cols[s][j] = cols[s][j] - (to_a * entry[a][j] + to_b * entry[b][j]) * inverse[a]
                rows[s] = rows[s] - (to_a * pivot_row[a] + to_b * pivot_row[b]) * inverse[a]
        for s in range(tiles):
            out = None
            for a in range(s * TILE, (s + 1) * TILE, 2):
                b = a + 1
                aa, ab, bb = entry[a][a], entry[a][b], entry[b][b]
                scale = lax.rsqrt(aa)
                first = pivot_row[a] * scale
                second = (pivot_row[b] * aa - pivot_row[a] * ab) * (scale * lax.rsqrt(aa * bb - ab * ab))
                out = first if out is None else jnp.where(subs == a % TILE, first, out)
                out = jnp.where(subs == b % TILE, second, out)
            done.append(out)
        if k + WINDOW == n:
            break
        solved = [None] * WINDOW
        for a in reversed(range(0, WINDOW, 2)):
            b = a + 1
            aa, ab, bb = entry[a][a], entry[a][b], entry[b][b]
            va, vb = pivot_row[a], pivot_row[b]
            for j in reversed(range(b + 1, WINDOW)):
                va, vb = va - entry[a][j] * solved[j], vb - entry[b][j] * solved[j]
            solved[a] = (bb * va - ab * vb) * inverse[a]
            solved[b] = (aa * vb - ab * va) * inverse[a]
        near = []
        for s in range(tiles):
            x = rest[s * TILE : (s + 1) * TILE]
            near.append(jnp.where(inside, 0.0, x) - total([column(x, k + j) * solved[j] for j in range(WINDOW)]))
        if k + 2 * WINDOW < n:
            x = rest[WINDOW:]
            pieces = [jnp.zeros((k, n), F32)] if k else []
            for s in range(tiles):
                tile = solved[s * TILE]
                for a in range(1, TILE):
                    tile = jnp.where(subs == a, solved[s * TILE + a], tile)
                pieces.append(tile)
            pieces.append(jnp.zeros((n - k - WINDOW, n), F32))
            rest = jnp.where(inside, 0.0, x) - dot3(split(x), split(jnp.concatenate(pieces, axis=0)), ROW_COL)
    r = lax.broadcasted_iota(jnp.int32, (n, n), 0)
    c = lax.broadcasted_iota(jnp.int32, (n, n), 1)
    return jnp.where(r >= c, jnp.concatenate(done, axis=0), 0.0)


def inverse_factor(m_ref, beside):
    n = m_ref.shape[0]
    tasks = []
    d = m_ref[:BLOCK, :BLOCK]
    for j, lo in enumerate(range(0, n, BLOCK)):
        hi = lo + BLOCK
        w = inverse_block(d, tasks + beside(j))
        ws = split(w)
        tasks = [functools.partial(finish_row, m_ref, lo, hi, w, ws)]
        if hi == n:
            break
        end = hi + BLOCK
        near = split(dot3(split(m_ref[hi:end, lo:hi]), ws, ROW_ROW))
        d = m_ref[hi:end, hi:end] - dot3(near, near, ROW_ROW)
        tasks += [functools.partial(finish_rows, m_ref, lo, hi, hi, end, near, None, ws)]
        if end < n:
            tasks += [functools.partial(finish_rows, m_ref, lo, hi, end, n, None, near, ws)]
    for task in tasks:
        task()


def equilibrate(m_ref, scale_ref):
    n = m_ref.shape[0]
    eye = lax.broadcasted_iota(jnp.int32, (BLOCK, BLOCK), 0) == lax.broadcasted_iota(jnp.int32, (BLOCK, BLOCK), 1)
    across = []
    for lo in range(0, n, BLOCK):
        hi = lo + BLOCK
        diagonal = jnp.where(eye, m_ref[lo:hi, lo:hi], 0.0)
        across.append(lax.rsqrt(jnp.sum(diagonal, axis=0, keepdims=True)))
        down = lax.rsqrt(jnp.sum(diagonal, axis=1, keepdims=True))
        scale_ref[:, lo:hi] = jnp.broadcast_to(across[-1], (TILE, BLOCK))
        for j, factor in enumerate(across):
            part = slice(j * BLOCK, (j + 1) * BLOCK)
            m_ref[lo:hi, part] = m_ref[lo:hi, part] * (down * factor)


def finish_row(m_ref, lo, hi, w, ws):
    if lo:
        m_ref[lo:hi, :lo] = dot3(ws, split(m_ref[lo:hi, :lo]), ROW_COL)
    m_ref[lo:hi, lo:hi] = w


def finish_rows(m_ref, lo, hi, start, end, factor, near, ws):
    if factor is None:
        factor = split(dot3(split(m_ref[start:end, lo:hi]), ws, ROW_ROW))
        m_ref[start:end, hi:start] = m_ref[start:end, hi:start] - dot3(factor, near, ROW_ROW)
        m_ref[start:end, start:end] = m_ref[start:end, start:end] - dot3(factor, factor, ROW_ROW)
    m_ref[start:end, lo:hi] = -dot3(factor, ws, ROW_COL)
    if lo:
        m_ref[start:end, :lo] = m_ref[start:end, :lo] - dot3(factor, split(m_ref[lo:hi, :lo]), ROW_COL)


def assemble(core, mine_ref, other_ref, gh_ref, gl_ref):
    size = gh_ref.shape[0] // GROUPS
    part = size // 2
    halves = ((mine_ref, core * part), (other_ref, (1 - core) * part))

    def place(value, row_at, col_at):
        where = pl.ds(pl.multiple_of(row_at, part), value.shape[0]), pl.ds(pl.multiple_of(col_at, part), value.shape[1])
        gh_ref[where], gl_ref[where] = split(value)

    for group in range(GROUPS):
        own, after = group * size, ((group + 1) % GROUPS) * size
        lo = group * 3 * size
        for ref, at in halves:
            place(ref[lo : lo + size, :], own, own + at)
            value = ref[lo + size : lo + 2 * size, :]
            place(value, after, own + at)
            place(value.T, own + at, after)
    for group in range(GROUPS // 2):
        after, last = (group + 1) * size, ((group - 1) % GROUPS) * size
        lo, opposite = (group * 3 + 2) * size, ((group + 2) * 3 + 2) * size
        for ref, at in halves:
            for ref_across, at_across in halves:
                value = ref[pl.ds(pl.multiple_of(lo + at_across, part), part), :]
                value = value + ref_across[pl.ds(pl.multiple_of(opposite + at, part), part), :].T
                place(value, after + at_across, last + at)
                place(value.T, last + at, after + at_across)


def iterate_kernel(
    iters, where_ref, mine_ref, other_ref, start_ref, out_ref, gh_ref, gl_ref, image_ref, ih_ref, il_ref, next_ref, m_ref, scale_ref
):
    assemble(where_ref[1], mine_ref, other_ref, gh_ref, gl_ref)
    n = m_ref.shape[0]
    half = n // 2
    image_ref[...] = dot3(split(start_ref[...]), (gh_ref[...], gl_ref[...]), ROW_COL)

    def orthonormalise(last):
        ih_ref[...], il_ref[...] = split(image_ref[...])
        for lo in (0, half):
            left = (ih_ref[lo : lo + half], il_ref[lo : lo + half])
            for to in range(0, lo + 1, half):
                right = (ih_ref[to : to + half], il_ref[to : to + half])
                m_ref[lo : lo + half, to : to + half] = dot3(left, right, ROW_ROW)

        def part_of_next(rows, cols):
            left = (ih_ref[rows, :], il_ref[rows, :])
            next_ref[rows, cols] = dot3(left, (gh_ref[:, cols], gl_ref[:, cols]), ROW_COL)

        def beside(j):
            if last:
                return []
            rows = pl.ds(j * BLOCK, BLOCK)
            width = 2 * BLOCK
            return [functools.partial(part_of_next, rows, pl.ds(at, width)) for at in range(0, gh_ref.shape[1], width)]

        equilibrate(m_ref, scale_ref)
        inverse_factor(m_ref, beside)

    def turn(i, carry):
        orthonormalise(False)
        high, low = split(next_ref[...])
        for lo in (0, half):
            hi = lo + half
            image_ref[lo:hi, :] = dot3(split(lower(m_ref, lo, hi) * scale_ref[:1, :hi]), (high[:hi], low[:hi]), ROW_COL)
        return carry

    lax.fori_loop(0, iters - 1, turn, 0)
    orthonormalise(True)
    cols = n // GROUPS
    at = pl.multiple_of(where_ref[0] * cols, cols)
    r = lax.broadcasted_iota(jnp.int32, (cols, n), 0) + at
    c = lax.broadcasted_iota(jnp.int32, (cols, n), 1)
    weights = split(jnp.where(r >= c, m_ref[pl.ds(at, cols), :], 0.0) * scale_ref[:1, :])
    basis = dot3(weights, (ih_ref[...], il_ref[...]), ROW_COL).astype(BF16)
    next_ref[:cols, :] = basis.astype(F32)
    size = out_ref.shape[1] // GROUPS
    for q in range(GROUPS):
        source = pl.multiple_of(lax.rem(where_ref[0] + q, GROUPS) * size, size)
        out_ref[:, q * size : (q + 1) * size] = next_ref[:cols, pl.ds(source, size)].astype(BF16)


def lower(m_ref, lo, hi):
    r = lax.broadcasted_iota(jnp.int32, (hi - lo, hi), 0) + lo
    c = lax.broadcasted_iota(jnp.int32, (hi - lo, hi), 1)
    return jnp.where(r >= c, m_ref[lo:hi, :hi], 0.0)


def iterate(where, mine, other, start, iters):
    k, n = start.shape
    return pl.pallas_call(
        functools.partial(iterate_kernel, iters),
        out_shape=jax.ShapeDtypeStruct((k // GROUPS, n), BF16),
        in_specs=[pl.BlockSpec(memory_space=pltpu.SMEM)] + [pl.BlockSpec(memory_space=pltpu.VMEM)] * 3,
        out_specs=pl.BlockSpec(memory_space=pltpu.VMEM),
        scratch_shapes=[
            pltpu.VMEM((n, n), BF16),
            pltpu.VMEM((n, n), BF16),
            pltpu.VMEM((k, n), F32),
            pltpu.VMEM((k, n), BF16),
            pltpu.VMEM((k, n), BF16),
            pltpu.VMEM((k, n), F32),
            pltpu.VMEM((k, k), F32),
            pltpu.VMEM((TILE, k), F32),
        ],
        compiler_params=pltpu.CompilerParams(vmem_limit_bytes=30 * 2**20),
        cost_estimate=pl.CostEstimate(flops=60 * 10**9, bytes_accessed=8 * 2**20, transcendentals=0),
    )(where, mine, other, start)


def modes_kernel(h, *refs):
    *whole, basis_ref, out_ref = refs
    across = whole.pop()
    inner, rims = whole[:3], whole[3:]
    rows = out_ref.shape[0]
    middle = rows - 2 * h
    size = basis_ref.shape[1] // GROUPS

    def project(refs, lo, hi, at):
        result = None
        for q, value in enumerate((refs[0][lo:hi, :], refs[1][lo:hi, :], across[at + lo : at + hi, :], refs[2][lo:hi, :])):
            part = basis_ref[:, q * size : (q + 1) * size]
            term = lax.dot_general(value, part, (ROW_ROW, ((), ())), preferred_element_type=F32)
            result = term if result is None else result + term
        return result

    out_ref[:h, :] = project(rims, 0, h, middle)
    out_ref[rows - h :, :] = project(rims, h, 2 * h, middle)
    out_ref[h : rows - h, :] = project(inner, 0, middle, 0)


def modes(own, following, across, behind, basis, rows, h):
    parts = [[p[i] for p in (own, following, behind)] for i in (0, 1)]
    return pl.pallas_call(
        functools.partial(modes_kernel, h),
        out_shape=jax.ShapeDtypeStruct((rows, basis.shape[0]), F32),
        in_specs=[pl.BlockSpec(memory_space=pltpu.VMEM)] * 8,
        out_specs=pl.BlockSpec(memory_space=pltpu.VMEM),
        compiler_params=pltpu.CompilerParams(vmem_limit_bytes=16 * 2**20),
    )(*parts[0], *parts[1], across, basis)


ITERS = 3
ROWS = ("y", "z", "core")


def neighbour_rims(top, bottom, core):
    blocks = lax.axis_size(ROWS)
    h = top.shape[0]
    zero = core == 0
    sibling = turn(jnp.where(zero, top, bottom), "core", 1)
    both = jnp.where(zero, jnp.concatenate([bottom, sibling]), jnp.concatenate([sibling, top]))
    pairs = [(i, i + 2 - 4 * (i % 2)) for i in range(blocks) if 0 <= i + 2 - 4 * (i % 2) < blocks]
    far = lax.ppermute(both, ROWS, pairs)
    handed = jnp.where(zero, jnp.concatenate([bottom, far[h:]]), jnp.concatenate([top, far[:h]]))
    given = turn(handed, "core", 1)
    below = jnp.where(zero, jnp.concatenate([far[h:], far[:h]]), given)
    above = jnp.where(zero, given, far)
    return below, above


def turn(value, axis, by):
    size = lax.axis_size(axis)
    return lax.ppermute(value, axis, [(i, (i + by) % size) for i in range(size)])


def spread(value, axis):
    size = 1
    for name in axis if isinstance(axis, tuple) else (axis,):
        size *= lax.axis_size(name)
    copies = jnp.broadcast_to(value[None], (size,) + value.shape).reshape((size * value.shape[0],) + value.shape[1:])
    return lax.all_to_all(copies, axis, 0, 0, tiled=True)


def cross(left, right):
    return lax.dot_general(left, right, (((0,), (0,)), ((), ())), preferred_element_type=F32)


def rim(snaps, mass, coupling, rims, offset):
    h = snaps.shape[0]
    other = jnp.where(offset == 1, rims[:h], rims[h:]).astype(F32)
    terms = jnp.dot(coupling, other, precision=lax.Precision.HIGHEST, preferred_element_type=F32)
    return (mass[:, None] * snaps.astype(F32) + terms).astype(BF16)


def shards(snapshots, mass_diag, lower_coupling, upper_coupling, band_offsets, start_basis):
    block_rows, width = snapshots.shape
    h = lower_coupling.shape[1]
    total_rows = block_rows * lax.axis_size(ROWS)
    group = lax.axis_index("x")
    core = lax.axis_index("core")

    inner = (mass_diag[h : block_rows - h, None] * snapshots[h : block_rows - h].astype(F32)).astype(BF16)
    top, bottom = snapshots[:h], snapshots[block_rows - h :]
    below, above = neighbour_rims(top, bottom, core)
    rims = jnp.concatenate(
        [
            rim(top, mass_diag[:h], lower_coupling[0], below, band_offsets[0, 0]),
            rim(bottom, mass_diag[block_rows - h :], upper_coupling[0], above, band_offsets[0, 1]),
        ],
        axis=0,
    )

    late = (group >= GROUPS // 2).astype(jnp.int32)

    def halved(piece):
        part = piece.shape[0] // 2
        return lax.dynamic_slice_in_dim(piece, late * part, part, 0)

    own = [inner, rims]
    following = [turn(piece, "x", -1) for piece in own]
    behind = [turn(piece, "x", 1) for piece in own]
    blocks = [
        sum(cross(p, p) for p in own),
        sum(cross(f, p) for f, p in zip(following, own)),
        sum(cross(halved(f), halved(p)) for f, p in zip(following, behind)),
    ]
    partial = jnp.concatenate(blocks, axis=0)
    forward = jnp.concatenate(following, axis=0)
    partial, start = lax.optimization_barrier((partial, start_basis.T))
    lanes = width // 2
    keep = lax.dynamic_slice_in_dim(partial, core * lanes, lanes, 1)
    give = lax.dynamic_slice_in_dim(partial, (1 - core) * lanes, lanes, 1)
    chip = keep + turn(give, "core", 1)
    sources = lax.axis_size(("y", "z"))
    pieces = lax.all_to_all(chip, ("y", "z"), 0, 0, tiled=True)
    share = pieces.reshape((sources, -1, lanes)).sum(0) / total_rows
    halves = spread(spread(share, "z"), ("x", "y"))
    other_halves = turn(halves, "core", 1)

    forward, halves, other_halves = lax.optimization_barrier((forward, halves, other_halves))
    across = turn(forward, "x", -1)
    where = jnp.stack([group, core]).astype(jnp.int32)
    basis = iterate(where, halves, other_halves, start, ITERS)
    return modes(own, following, across, behind, basis, block_rows, h)


def solution(mesh):
    fine = jax.sharding.Mesh(mesh.devices.reshape(4, 8, 2, 4), ("y", "z", "core", "x"))
    placed = (
        P(ROWS, "x"),
        P(ROWS),
        P(ROWS, None, None),
        P(ROWS, None, None),
        P(ROWS, None),
        P(),
    )
    return jax.shard_map(shards, mesh=fine, in_specs=placed, out_specs=P(ROWS, "x"), check_vma=False)
```

```python
import functools

import jax
import jax.numpy as jnp
from jax import lax
from jax.experimental import pallas as pl
from jax.experimental.pallas import tpu as pltpu
from jax.sharding import PartitionSpec as P

F32 = jnp.float32
BF16 = jnp.bfloat16
GROUPS = 4
BLOCK = 128
TILE = 8
WINDOW = 16
ROW_COL = ((1,), (0,))
ROW_ROW = ((1,), (1,))


def split(value):
    high = value.astype(BF16)
    return high, (value - high.astype(F32)).astype(BF16)


def dot3(left, right, dims):
    one = lambda a, b: lax.dot_general(a, b, (dims, ((), ())), preferred_element_type=F32)
    return one(left[0], right[0]) + (one(left[0], right[1]) + one(left[1], right[0]))


def row(tile, index):
    return jnp.broadcast_to(tile[index : index + 1], tile.shape)


def column(tile, index):
    return jnp.broadcast_to(tile[:, index : index + 1], tile.shape)


def total(terms):
    while len(terms) > 1:
        terms = [sum(terms[i : i + 2][1:], terms[i]) for i in range(0, len(terms), 2)]
    return terms[0]


def inverse_block(m, beside):
    n = m.shape[0]
    tiles = WINDOW // TILE
    lanes = lax.broadcasted_iota(jnp.int32, (1, n), 1)
    subs = lax.broadcasted_iota(jnp.int32, (TILE, n), 0)
    done = []
    near = [m[s * TILE : (s + 1) * TILE] for s in range(tiles)]
    rest = m[WINDOW:]
    for k in range(0, n, WINDOW):
        for _ in range(-(-len(beside) * WINDOW // (n - k))):
            beside.pop(0)()
        inside = (lanes >= k) & (lanes < k + WINDOW)
        cols = [[column(near[s], k + j) for j in range((s + 1) * TILE)] for s in range(tiles)]
        rows = [
            jnp.where(inside, jnp.where(lanes == subs + (k + s * TILE), 1.0, 0.0), near[s]) for s in range(tiles)
        ]
        entry, pivot_row, inverse = {}, {}, {}
        for a in range(0, WINDOW, 2):
            b, t = a + 1, a // TILE
            for p in (a, b):
                entry[p] = {j: row(cols[j // TILE][p], j % TILE) for j in range(p, WINDOW)}
                pivot_row[p] = row(rows[t], p % TILE)
            aa, ab, bb = entry[a][a], entry[a][b], entry[b][b]
            inverse[a] = 1.0 / (aa * bb - ab * ab)
            for s in range(t, tiles):
                if s == t and b % TILE == TILE - 1:
                    continue
                to_a = cols[s][a] * bb - cols[s][b] * ab
                to_b = cols[s][b] * aa - cols[s][a] * ab
                if s == t:
                    later = subs > b % TILE
                    to_a, to_b = jnp.where(later, to_a, 0.0), jnp.where(later, to_b, 0.0)
                for j in range(b + 1, (s + 1) * TILE):
                    cols[s][j] = cols[s][j] - (to_a * entry[a][j] + to_b * entry[b][j]) * inverse[a]
                rows[s] = rows[s] - (to_a * pivot_row[a] + to_b * pivot_row[b]) * inverse[a]
        for s in range(tiles):
            out = None
            for a in range(s * TILE, (s + 1) * TILE, 2):
                b = a + 1
                aa, ab, bb = entry[a][a], entry[a][b], entry[b][b]
                scale = lax.rsqrt(aa)
                first = pivot_row[a] * scale
                second = (pivot_row[b] * aa - pivot_row[a] * ab) * (scale * lax.rsqrt(aa * bb - ab * ab))
                out = first if out is None else jnp.where(subs == a % TILE, first, out)
                out = jnp.where(subs == b % TILE, second, out)
            done.append(out)
        if k + WINDOW == n:
            break
        solved = [None] * WINDOW
        for a in reversed(range(0, WINDOW, 2)):
            b = a + 1
            aa, ab, bb = entry[a][a], entry[a][b], entry[b][b]
            va, vb = pivot_row[a], pivot_row[b]
            for j in reversed(range(b + 1, WINDOW)):
                va, vb = va - entry[a][j] * solved[j], vb - entry[b][j] * solved[j]
            solved[a] = (bb * va - ab * vb) * inverse[a]
            solved[b] = (aa * vb - ab * va) * inverse[a]
        near = []
        for s in range(tiles):
            x = rest[s * TILE : (s + 1) * TILE]
            near.append(jnp.where(inside, 0.0, x) - total([column(x, k + j) * solved[j] for j in range(WINDOW)]))
        if k + 2 * WINDOW < n:
            x = rest[WINDOW:]
            pieces = [jnp.zeros((k, n), F32)] if k else []
            for s in range(tiles):
                tile = solved[s * TILE]
                for a in range(1, TILE):
                    tile = jnp.where(subs == a, solved[s * TILE + a], tile)
                pieces.append(tile)
            pieces.append(jnp.zeros((n - k - WINDOW, n), F32))
            rest = jnp.where(inside, 0.0, x) - dot3(split(x), split(jnp.concatenate(pieces, axis=0)), ROW_COL)
    r = lax.broadcasted_iota(jnp.int32, (n, n), 0)
    c = lax.broadcasted_iota(jnp.int32, (n, n), 1)
    return jnp.where(r >= c, jnp.concatenate(done, axis=0), 0.0)


def inverse_factor(m_ref, beside):
    n = m_ref.shape[0]
    tasks = []
    d = m_ref[:BLOCK, :BLOCK]
    for j, lo in enumerate(range(0, n, BLOCK)):
        hi = lo + BLOCK
        w = inverse_block(d, tasks + beside(j))
        ws = split(w)
        tasks = [functools.partial(finish_row, m_ref, lo, hi, w, ws)]
        if hi == n:
            break
        end = hi + BLOCK
        near = split(dot3(split(m_ref[hi:end, lo:hi]), ws, ROW_ROW))
        d = m_ref[hi:end, hi:end] - dot3(near, near, ROW_ROW)
        tasks += [functools.partial(finish_rows, m_ref, lo, hi, hi, end, near, None, ws)]
        if end < n:
            tasks += [functools.partial(finish_rows, m_ref, lo, hi, end, n, None, near, ws)]
    for task in tasks:
        task()


def equilibrate(m_ref, scale_ref):
    n = m_ref.shape[0]
    eye = lax.broadcasted_iota(jnp.int32, (BLOCK, BLOCK), 0) == lax.broadcasted_iota(jnp.int32, (BLOCK, BLOCK), 1)
    across = []
    for lo in range(0, n, BLOCK):
        hi = lo + BLOCK
        diagonal = jnp.where(eye, m_ref[lo:hi, lo:hi], 0.0)
        across.append(lax.rsqrt(jnp.sum(diagonal, axis=0, keepdims=True)))
        down = lax.rsqrt(jnp.sum(diagonal, axis=1, keepdims=True))
        scale_ref[:, lo:hi] = jnp.broadcast_to(across[-1], (TILE, BLOCK))
        for j, factor in enumerate(across):
            part = slice(j * BLOCK, (j + 1) * BLOCK)
            m_ref[lo:hi, part] = m_ref[lo:hi, part] * (down * factor)


def finish_row(m_ref, lo, hi, w, ws):
    if lo:
        m_ref[lo:hi, :lo] = dot3(ws, split(m_ref[lo:hi, :lo]), ROW_COL)
    m_ref[lo:hi, lo:hi] = w


def finish_rows(m_ref, lo, hi, start, end, factor, near, ws):
    if factor is None:
        factor = split(dot3(split(m_ref[start:end, lo:hi]), ws, ROW_ROW))
        m_ref[start:end, hi:start] = m_ref[start:end, hi:start] - dot3(factor, near, ROW_ROW)
        m_ref[start:end, start:end] = m_ref[start:end, start:end] - dot3(factor, factor, ROW_ROW)
    m_ref[start:end, lo:hi] = -dot3(factor, ws, ROW_COL)
    if lo:
        m_ref[start:end, :lo] = m_ref[start:end, :lo] - dot3(factor, split(m_ref[lo:hi, :lo]), ROW_COL)


def assemble(core, mine_ref, other_ref, gh_ref, gl_ref):
    size = gh_ref.shape[0] // GROUPS
    part = size // 2
    halves = ((mine_ref, core * part), (other_ref, (1 - core) * part))

    def place(value, row_at, col_at):
        where = pl.ds(pl.multiple_of(row_at, part), value.shape[0]), pl.ds(pl.multiple_of(col_at, part), value.shape[1])
        gh_ref[where], gl_ref[where] = split(value)

    for group in range(GROUPS):
        own, after = group * size, ((group + 1) % GROUPS) * size
        lo = group * 3 * size
        for ref, at in halves:
            place(ref[lo : lo + size, :], own, own + at)
            value = ref[lo + size : lo + 2 * size, :]
            place(value, after, own + at)
            place(value.T, own + at, after)
    for group in range(GROUPS // 2):
        after, last = (group + 1) * size, ((group - 1) % GROUPS) * size
        lo, opposite = (group * 3 + 2) * size, ((group + 2) * 3 + 2) * size
        for ref, at in halves:
            for ref_across, at_across in halves:
                value = ref[pl.ds(pl.multiple_of(lo + at_across, part), part), :]
                value = value + ref_across[pl.ds(pl.multiple_of(opposite + at, part), part), :].T
                place(value, after + at_across, last + at)
                place(value.T, last + at, after + at_across)


def iterate_kernel(
    iters, where_ref, mine_ref, other_ref, start_ref, out_ref, gh_ref, gl_ref, image_ref, ih_ref, il_ref, next_ref, m_ref, scale_ref
):
    assemble(where_ref[1], mine_ref, other_ref, gh_ref, gl_ref)
    n = m_ref.shape[0]
    half = n // 2
    image_ref[...] = dot3(split(start_ref[...]), (gh_ref[...], gl_ref[...]), ROW_COL)

    def orthonormalise(i, carry):
        @pl.when(i > 0)
        def _():
            high, low = split(next_ref[...])
            for lo in (0, half):
                hi = lo + half
                weights = split(lower(m_ref, lo, hi) * scale_ref[:1, :hi])
                image_ref[lo:hi, :] = dot3(weights, (high[:hi], low[:hi]), ROW_COL)

        ih_ref[...], il_ref[...] = split(image_ref[...])
        for lo in (0, half):
            left = (ih_ref[lo : lo + half], il_ref[lo : lo + half])
            for to in range(0, lo + 1, half):
                right = (ih_ref[to : to + half], il_ref[to : to + half])
                m_ref[lo : lo + half, to : to + half] = dot3(left, right, ROW_ROW)

        def part_of_next(rows, cols):
            left = (ih_ref[rows, :], il_ref[rows, :])
            next_ref[rows, cols] = dot3(left, (gh_ref[:, cols], gl_ref[:, cols]), ROW_COL)

        def beside(j):
            rows = pl.ds(j * BLOCK, BLOCK)
            width = 2 * BLOCK
            return [functools.partial(part_of_next, rows, pl.ds(at, width)) for at in range(0, gh_ref.shape[1], width)]

        equilibrate(m_ref, scale_ref)
        inverse_factor(m_ref, beside)
        return carry

    lax.fori_loop(0, iters, orthonormalise, 0)
    cols = n // GROUPS
    at = pl.multiple_of(where_ref[0] * cols, cols)
    r = lax.broadcasted_iota(jnp.int32, (cols, n), 0) + at
    c = lax.broadcasted_iota(jnp.int32, (cols, n), 1)
    weights = split(jnp.where(r >= c, m_ref[pl.ds(at, cols), :], 0.0) * scale_ref[:1, :])
    basis = dot3(weights, (ih_ref[...], il_ref[...]), ROW_COL).astype(BF16)
    next_ref[:cols, :] = basis.astype(F32)
    size = out_ref.shape[1] // GROUPS
    for q in range(GROUPS):
        source = pl.multiple_of(lax.rem(where_ref[0] + q, GROUPS) * size, size)
        out_ref[:, q * size : (q + 1) * size] = next_ref[:cols, pl.ds(source, size)].astype(BF16)


def lower(m_ref, lo, hi):
    r = lax.broadcasted_iota(jnp.int32, (hi - lo, hi), 0) + lo
    c = lax.broadcasted_iota(jnp.int32, (hi - lo, hi), 1)
    return jnp.where(r >= c, m_ref[lo:hi, :hi], 0.0)


def iterate(where, mine, other, start, iters):
    k, n = start.shape
    return pl.pallas_call(
        functools.partial(iterate_kernel, iters),
        out_shape=jax.ShapeDtypeStruct((k // GROUPS, n), BF16),
        in_specs=[pl.BlockSpec(memory_space=pltpu.SMEM)] + [pl.BlockSpec(memory_space=pltpu.VMEM)] * 3,
        out_specs=pl.BlockSpec(memory_space=pltpu.VMEM),
        scratch_shapes=[
            pltpu.VMEM((n, n), BF16),
            pltpu.VMEM((n, n), BF16),
            pltpu.VMEM((k, n), F32),
            pltpu.VMEM((k, n), BF16),
            pltpu.VMEM((k, n), BF16),
            pltpu.VMEM((k, n), F32),
            pltpu.VMEM((k, k), F32),
            pltpu.VMEM((TILE, k), F32),
        ],
        compiler_params=pltpu.CompilerParams(vmem_limit_bytes=30 * 2**20),
        cost_estimate=pl.CostEstimate(flops=10**6, bytes_accessed=2**20, transcendentals=0),
    )(where, mine, other, start)


def modes_kernel(h, *refs):
    *whole, basis_ref, out_ref = refs
    across = whole.pop()
    inner, rims = whole[:3], whole[3:]
    rows = out_ref.shape[0]
    middle = rows - 2 * h
    size = basis_ref.shape[1] // GROUPS

    def project(refs, lo, hi, at):
        result = None
        for q, value in enumerate((refs[0][lo:hi, :], refs[1][lo:hi, :], across[at + lo : at + hi, :], refs[2][lo:hi, :])):
            part = basis_ref[:, q * size : (q + 1) * size]
            term = lax.dot_general(value, part, (ROW_ROW, ((), ())), preferred_element_type=F32)
            result = term if result is None else result + term
        return result

    out_ref[:h, :] = project(rims, 0, h, middle)
    out_ref[rows - h :, :] = project(rims, h, 2 * h, middle)
    out_ref[h : rows - h, :] = project(inner, 0, middle, 0)


def modes(own, following, across, behind, basis, rows, h):
    parts = [[p[i] for p in (own, following, behind)] for i in (0, 1)]
    return pl.pallas_call(
        functools.partial(modes_kernel, h),
        out_shape=jax.ShapeDtypeStruct((rows, basis.shape[0]), F32),
        in_specs=[pl.BlockSpec(memory_space=pltpu.VMEM)] * 8,
        out_specs=pl.BlockSpec(memory_space=pltpu.VMEM),
        compiler_params=pltpu.CompilerParams(vmem_limit_bytes=16 * 2**20),
    )(*parts[0], *parts[1], across, basis)


ITERS = 3
ROWS = ("y", "z", "core")


def neighbour_rims(top, bottom, core):
    blocks = lax.axis_size(ROWS)
    h = top.shape[0]
    zero = core == 0
    sibling = turn(jnp.where(zero, top, bottom), "core", 1)
    both = jnp.where(zero, jnp.concatenate([bottom, sibling]), jnp.concatenate([sibling, top]))
    pairs = [(i, i + 2 - 4 * (i % 2)) for i in range(blocks) if 0 <= i + 2 - 4 * (i % 2) < blocks]
    far = lax.ppermute(both, ROWS, pairs)
    handed = jnp.where(zero, jnp.concatenate([bottom, far[h:]]), jnp.concatenate([top, far[:h]]))
    given = turn(handed, "core", 1)
    below = jnp.where(zero, jnp.concatenate([far[h:], far[:h]]), given)
    above = jnp.where(zero, given, far)
    return below, above


def turn(value, axis, by):
    size = lax.axis_size(axis)
    return lax.ppermute(value, axis, [(i, (i + by) % size) for i in range(size)])


def spread(value, axis):
    size = 1
    for name in axis if isinstance(axis, tuple) else (axis,):
        size *= lax.axis_size(name)
    copies = jnp.broadcast_to(value[None], (size,) + value.shape).reshape((size * value.shape[0],) + value.shape[1:])
    return lax.all_to_all(copies, axis, 0, 0, tiled=True)


def cross(left, right):
    return lax.dot_general(left, right, (((0,), (0,)), ((), ())), preferred_element_type=F32)


def rim(snaps, mass, coupling, rims, offset):
    h = snaps.shape[0]
    other = jnp.where(offset == 1, rims[:h], rims[h:]).astype(F32)
    terms = jnp.dot(coupling, other, precision=lax.Precision.HIGHEST, preferred_element_type=F32)
    return (mass[:, None] * snaps.astype(F32) + terms).astype(BF16)


def shards(snapshots, mass_diag, lower_coupling, upper_coupling, band_offsets, start_basis):
    block_rows, width = snapshots.shape
    h = lower_coupling.shape[1]
    total_rows = block_rows * lax.axis_size(ROWS)
    group = lax.axis_index("x")
    core = lax.axis_index("core")

    inner = (mass_diag[h : block_rows - h, None] * snapshots[h : block_rows - h].astype(F32)).astype(BF16)
    top, bottom = snapshots[:h], snapshots[block_rows - h :]
    below, above = neighbour_rims(top, bottom, core)
    rims = jnp.concatenate(
        [
            rim(top, mass_diag[:h], lower_coupling[0], below, band_offsets[0, 0]),
            rim(bottom, mass_diag[block_rows - h :], upper_coupling[0], above, band_offsets[0, 1]),
        ],
        axis=0,
    )

    late = (group >= GROUPS // 2).astype(jnp.int32)

    def halved(piece):
        part = piece.shape[0] // 2
        return lax.dynamic_slice_in_dim(piece, late * part, part, 0)

    own = [inner, rims]
    following = [turn(piece, "x", -1) for piece in own]
    behind = [turn(piece, "x", 1) for piece in own]
    blocks = [
        sum(cross(p, p) for p in own),
        sum(cross(f, p) for f, p in zip(following, own)),
        sum(cross(halved(f), halved(p)) for f, p in zip(following, behind)),
    ]
    partial = jnp.concatenate(blocks, axis=0)
    forward = jnp.concatenate(following, axis=0)
    partial, start = lax.optimization_barrier((partial, start_basis.T))
    lanes = width // 2
    keep = lax.dynamic_slice_in_dim(partial, core * lanes, lanes, 1)
    give = lax.dynamic_slice_in_dim(partial, (1 - core) * lanes, lanes, 1)
    chip = keep + turn(give, "core", 1)
    across = turn(forward, "x", -1)
    sources = lax.axis_size(("y", "z"))
    pieces = lax.all_to_all(chip, ("y", "z"), 0, 0, tiled=True)
    share = pieces.reshape((sources, -1, lanes)).sum(0) / total_rows
    halves = spread(spread(share, "z"), ("x", "y"))
    other_halves = turn(halves, "core", 1)

    where = jnp.stack([group, core]).astype(jnp.int32)
    basis = iterate(where, halves, other_halves, start, ITERS)
    return modes(own, following, across, behind, basis, block_rows, h)


def solution(mesh):
    fine = jax.sharding.Mesh(mesh.devices.reshape(4, 8, 2, 4), ("y", "z", "core", "x"))
    placed = (
        P(ROWS, "x"),
        P(ROWS),
        P(ROWS, None, None),
        P(ROWS, None, None),
        P(ROWS, None),
        P(),
    )
    return jax.shard_map(shards, mesh=fine, in_specs=placed, out_specs=P(ROWS, "x"), check_vma=False)
```

```python
import functools

import jax
import jax.numpy as jnp
from jax import lax
from jax.experimental import pallas as pl
from jax.experimental.pallas import tpu as pltpu
from jax.sharding import PartitionSpec as P

F32 = jnp.float32
BF16 = jnp.bfloat16
GROUPS = 4
BLOCK = 128
TILE = 8
WINDOW = 16
ROW_COL = ((1,), (0,))
ROW_ROW = ((1,), (1,))


def split(value):
    high = value.astype(BF16)
    return high, (value - high.astype(F32)).astype(BF16)


def dot3(left, right, dims):
    one = lambda a, b: lax.dot_general(a, b, (dims, ((), ())), preferred_element_type=F32)
    return one(left[0], right[0]) + (one(left[0], right[1]) + one(left[1], right[0]))


def row(tile, index):
    return jnp.broadcast_to(tile[index : index + 1], tile.shape)


def column(tile, index):
    return jnp.broadcast_to(tile[:, index : index + 1], tile.shape)


def total(terms):
    while len(terms) > 1:
        terms = [sum(terms[i : i + 2][1:], terms[i]) for i in range(0, len(terms), 2)]
    return terms[0]


def inverse_block(m, beside):
    n = m.shape[0]
    tiles = WINDOW // TILE
    lanes = lax.broadcasted_iota(jnp.int32, (1, n), 1)
    subs = lax.broadcasted_iota(jnp.int32, (TILE, n), 0)
    done = []
    near = [m[s * TILE : (s + 1) * TILE] for s in range(tiles)]
    rest = m[WINDOW:]
    for k in range(0, n, WINDOW):
        for _ in range(-(-len(beside) * WINDOW // (n - k))):
            beside.pop(0)()
        inside = (lanes >= k) & (lanes < k + WINDOW)
        cols = [[column(near[s], k + j) for j in range((s + 1) * TILE)] for s in range(tiles)]
        rows = [
            jnp.where(inside, jnp.where(lanes == subs + (k + s * TILE), 1.0, 0.0), near[s]) for s in range(tiles)
        ]
        entry, pivot_row, inverse = {}, {}, {}
        for a in range(0, WINDOW, 2):
            b, t = a + 1, a // TILE
            for p in (a, b):
                entry[p] = {j: row(cols[j // TILE][p], j % TILE) for j in range(p, WINDOW)}
                pivot_row[p] = row(rows[t], p % TILE)
            aa, ab, bb = entry[a][a], entry[a][b], entry[b][b]
            inverse[a] = 1.0 / (aa * bb - ab * ab)
            for s in range(t, tiles):
                if s == t and b % TILE == TILE - 1:
                    continue
                to_a = cols[s][a] * bb - cols[s][b] * ab
                to_b = cols[s][b] * aa - cols[s][a] * ab
                if s == t:
                    later = subs > b % TILE
                    to_a, to_b = jnp.where(later, to_a, 0.0), jnp.where(later, to_b, 0.0)
                for j in range(b + 1, (s + 1) * TILE):
                    cols[s][j] = cols[s][j] - (to_a * entry[a][j] + to_b * entry[b][j]) * inverse[a]
                rows[s] = rows[s] - (to_a * pivot_row[a] + to_b * pivot_row[b]) * inverse[a]
        for s in range(tiles):
            out = None
            for a in range(s * TILE, (s + 1) * TILE, 2):
                b = a + 1
                aa, ab, bb = entry[a][a], entry[a][b], entry[b][b]
                scale = lax.rsqrt(aa)
                first = pivot_row[a] * scale
                second = (pivot_row[b] * aa - pivot_row[a] * ab) * (scale * lax.rsqrt(aa * bb - ab * ab))
                out = first if out is None else jnp.where(subs == a % TILE, first, out)
                out = jnp.where(subs == b % TILE, second, out)
            done.append(out)
        if k + WINDOW == n:
            break
        solved = [None] * WINDOW
        for a in reversed(range(0, WINDOW, 2)):
            b = a + 1
            aa, ab, bb = entry[a][a], entry[a][b], entry[b][b]
            va, vb = pivot_row[a], pivot_row[b]
            for j in reversed(range(b + 1, WINDOW)):
                va, vb = va - entry[a][j] * solved[j], vb - entry[b][j] * solved[j]
            solved[a] = (bb * va - ab * vb) * inverse[a]
            solved[b] = (aa * vb - ab * va) * inverse[a]
        near = []
        for s in range(tiles):
            x = rest[s * TILE : (s + 1) * TILE]
            near.append(jnp.where(inside, 0.0, x) - total([column(x, k + j) * solved[j] for j in range(WINDOW)]))
        if k + 2 * WINDOW < n:
            x = rest[WINDOW:]
            pieces = [jnp.zeros((k, n), F32)] if k else []
            for s in range(tiles):
                tile = solved[s * TILE]
                for a in range(1, TILE):
                    tile = jnp.where(subs == a, solved[s * TILE + a], tile)
                pieces.append(tile)
            pieces.append(jnp.zeros((n - k - WINDOW, n), F32))
            rest = jnp.where(inside, 0.0, x) - dot3(split(x), split(jnp.concatenate(pieces, axis=0)), ROW_COL)
    r = lax.broadcasted_iota(jnp.int32, (n, n), 0)
    c = lax.broadcasted_iota(jnp.int32, (n, n), 1)
    return jnp.where(r >= c, jnp.concatenate(done, axis=0), 0.0)


def inverse_factor(m_ref, beside):
    n = m_ref.shape[0]
    tasks = []
    d = m_ref[:BLOCK, :BLOCK]
    for j, lo in enumerate(range(0, n, BLOCK)):
        hi = lo + BLOCK
        w = inverse_block(d, tasks + beside(j))
        ws = split(w)
        tasks = [functools.partial(finish_row, m_ref, lo, hi, w, ws)]
        if hi == n:
            break
        end = hi + BLOCK
        near = split(dot3(split(m_ref[hi:end, lo:hi]), ws, ROW_ROW))
        d = m_ref[hi:end, hi:end] - dot3(near, near, ROW_ROW)
        tasks += [functools.partial(finish_rows, m_ref, lo, hi, hi, end, near, None, ws)]
        if end < n:
            tasks += [functools.partial(finish_rows, m_ref, lo, hi, end, n, None, near, ws)]
    for task in tasks:
        task()


def equilibrate(m_ref, scale_ref):
    n = m_ref.shape[0]
    eye = lax.broadcasted_iota(jnp.int32, (BLOCK, BLOCK), 0) == lax.broadcasted_iota(jnp.int32, (BLOCK, BLOCK), 1)
    across = []
    for lo in range(0, n, BLOCK):
        hi = lo + BLOCK
        diagonal = jnp.where(eye, m_ref[lo:hi, lo:hi], 0.0)
        across.append(lax.rsqrt(jnp.sum(diagonal, axis=0, keepdims=True)))
        down = lax.rsqrt(jnp.sum(diagonal, axis=1, keepdims=True))
        scale_ref[:, lo:hi] = jnp.broadcast_to(across[-1], (TILE, BLOCK))
        for j, factor in enumerate(across):
            part = slice(j * BLOCK, (j + 1) * BLOCK)
            m_ref[lo:hi, part] = m_ref[lo:hi, part] * (down * factor)


def finish_row(m_ref, lo, hi, w, ws):
    if lo:
        m_ref[lo:hi, :lo] = dot3(ws, split(m_ref[lo:hi, :lo]), ROW_COL)
    m_ref[lo:hi, lo:hi] = w


def finish_rows(m_ref, lo, hi, start, end, factor, near, ws):
    if factor is None:
        factor = split(dot3(split(m_ref[start:end, lo:hi]), ws, ROW_ROW))
        m_ref[start:end, hi:start] = m_ref[start:end, hi:start] - dot3(factor, near, ROW_ROW)
        m_ref[start:end, start:end] = m_ref[start:end, start:end] - dot3(factor, factor, ROW_ROW)
    m_ref[start:end, lo:hi] = -dot3(factor, ws, ROW_COL)
    if lo:
        m_ref[start:end, :lo] = m_ref[start:end, :lo] - dot3(factor, split(m_ref[lo:hi, :lo]), ROW_COL)


def assemble(core, mine_ref, other_ref, gh_ref, gl_ref):
    size = gh_ref.shape[0] // GROUPS
    part = size // 2
    halves = ((mine_ref, core * part), (other_ref, (1 - core) * part))

    def place(value, row_at, col_at):
        where = pl.ds(pl.multiple_of(row_at, part), value.shape[0]), pl.ds(pl.multiple_of(col_at, part), value.shape[1])
        gh_ref[where], gl_ref[where] = split(value)

    for group in range(GROUPS):
        own, after = group * size, ((group + 1) % GROUPS) * size
        lo = group * 3 * size
        for ref, at in halves:
            place(ref[lo : lo + size, :], own, own + at)
            value = ref[lo + size : lo + 2 * size, :]
            place(value, after, own + at)
            place(value.T, own + at, after)
    for group in range(GROUPS // 2):
        after, last = (group + 1) * size, ((group - 1) % GROUPS) * size
        lo, opposite = (group * 3 + 2) * size, ((group + 2) * 3 + 2) * size
        for ref, at in halves:
            for ref_across, at_across in halves:
                value = ref[pl.ds(pl.multiple_of(lo + at_across, part), part), :]
                value = value + ref_across[pl.ds(pl.multiple_of(opposite + at, part), part), :].T
                place(value, after + at_across, last + at)
                place(value.T, last + at, after + at_across)


def iterate_kernel(
    iters, where_ref, mine_ref, other_ref, start_ref, out_ref, gh_ref, gl_ref, image_ref, ih_ref, il_ref, next_ref, m_ref, scale_ref
):
    assemble(where_ref[1], mine_ref, other_ref, gh_ref, gl_ref)
    n = m_ref.shape[0]
    half = n // 2
    image_ref[...] = dot3(split(start_ref[...]), (gh_ref[...], gl_ref[...]), ROW_COL)

    def orthonormalise(i, carry):
        @pl.when(i > 0)
        def _():
            high, low = split(next_ref[...])
            for lo in (0, half):
                hi = lo + half
                weights = split(lower(m_ref, lo, hi) * scale_ref[:1, :hi])
                image_ref[lo:hi, :] = dot3(weights, (high[:hi], low[:hi]), ROW_COL)

        ih_ref[...], il_ref[...] = split(image_ref[...])
        for lo in (0, half):
            left = (ih_ref[lo : lo + half], il_ref[lo : lo + half])
            for to in range(0, lo + 1, half):
                right = (ih_ref[to : to + half], il_ref[to : to + half])
                m_ref[lo : lo + half, to : to + half] = dot3(left, right, ROW_ROW)

        def part_of_next(rows, cols):
            left = (ih_ref[rows, :], il_ref[rows, :])
            next_ref[rows, cols] = dot3(left, (gh_ref[:, cols], gl_ref[:, cols]), ROW_COL)

        def beside(j):
            rows = pl.ds(j * BLOCK, BLOCK)
            width = 2 * BLOCK
            return [functools.partial(part_of_next, rows, pl.ds(at, width)) for at in range(0, gh_ref.shape[1], width)]

        equilibrate(m_ref, scale_ref)
        inverse_factor(m_ref, beside)
        return carry

    lax.fori_loop(0, iters, orthonormalise, 0)
    cols = n // GROUPS
    at = pl.multiple_of(where_ref[0] * cols, cols)
    r = lax.broadcasted_iota(jnp.int32, (cols, n), 0) + at
    c = lax.broadcasted_iota(jnp.int32, (cols, n), 1)
    weights = split(jnp.where(r >= c, m_ref[pl.ds(at, cols), :], 0.0) * scale_ref[:1, :])
    basis = dot3(weights, (ih_ref[...], il_ref[...]), ROW_COL).astype(BF16)
    next_ref[:cols, :] = basis.astype(F32)
    size = out_ref.shape[1] // GROUPS
    for q in range(GROUPS):
        source = pl.multiple_of(lax.rem(where_ref[0] + q, GROUPS) * size, size)
        out_ref[:, q * size : (q + 1) * size] = next_ref[:cols, pl.ds(source, size)].astype(BF16)


def lower(m_ref, lo, hi):
    r = lax.broadcasted_iota(jnp.int32, (hi - lo, hi), 0) + lo
    c = lax.broadcasted_iota(jnp.int32, (hi - lo, hi), 1)
    return jnp.where(r >= c, m_ref[lo:hi, :hi], 0.0)


def iterate(where, mine, other, start, iters):
    k, n = start.shape
    return pl.pallas_call(
        functools.partial(iterate_kernel, iters),
        out_shape=jax.ShapeDtypeStruct((k // GROUPS, n), BF16),
        in_specs=[pl.BlockSpec(memory_space=pltpu.SMEM)] + [pl.BlockSpec(memory_space=pltpu.VMEM)] * 3,
        out_specs=pl.BlockSpec(memory_space=pltpu.VMEM),
        scratch_shapes=[
            pltpu.VMEM((n, n), BF16),
            pltpu.VMEM((n, n), BF16),
            pltpu.VMEM((k, n), F32),
            pltpu.VMEM((k, n), BF16),
            pltpu.VMEM((k, n), BF16),
            pltpu.VMEM((k, n), F32),
            pltpu.VMEM((k, k), F32),
            pltpu.VMEM((TILE, k), F32),
        ],
        compiler_params=pltpu.CompilerParams(vmem_limit_bytes=30 * 2**20),
        cost_estimate=pl.CostEstimate(flops=10**6, bytes_accessed=2**20, transcendentals=0),
    )(where, mine, other, start)


def modes_kernel(h, *refs):
    *whole, basis_ref, out_ref = refs
    across = whole.pop()
    inner, rims = whole[:3], whole[3:]
    rows = out_ref.shape[0]
    middle = rows - 2 * h
    size = basis_ref.shape[1] // GROUPS

    def project(refs, lo, hi, at):
        result = None
        for q, value in enumerate((refs[0][lo:hi, :], refs[1][lo:hi, :], across[at + lo : at + hi, :], refs[2][lo:hi, :])):
            part = basis_ref[:, q * size : (q + 1) * size]
            term = lax.dot_general(value, part, (ROW_ROW, ((), ())), preferred_element_type=F32)
            result = term if result is None else result + term
        return result

    out_ref[:h, :] = project(rims, 0, h, middle)
    out_ref[rows - h :, :] = project(rims, h, 2 * h, middle)
    out_ref[h : rows - h, :] = project(inner, 0, middle, 0)


def modes(own, following, across, behind, basis, rows, h):
    parts = [[p[i] for p in (own, following, behind)] for i in (0, 1)]
    return pl.pallas_call(
        functools.partial(modes_kernel, h),
        out_shape=jax.ShapeDtypeStruct((rows, basis.shape[0]), F32),
        in_specs=[pl.BlockSpec(memory_space=pltpu.VMEM)] * 8,
        out_specs=pl.BlockSpec(memory_space=pltpu.VMEM),
        compiler_params=pltpu.CompilerParams(vmem_limit_bytes=16 * 2**20),
    )(*parts[0], *parts[1], across, basis)


ITERS = 3
ROWS = ("y", "z", "core")


def neighbour_rims(top, bottom, core):
    blocks = lax.axis_size(ROWS)
    h = top.shape[0]
    zero = core == 0
    sibling = turn(jnp.where(zero, top, bottom), "core", 1)
    both = jnp.where(zero, jnp.concatenate([bottom, sibling]), jnp.concatenate([sibling, top]))
    pairs = [(i, i + 2 - 4 * (i % 2)) for i in range(blocks) if 0 <= i + 2 - 4 * (i % 2) < blocks]
    far = lax.ppermute(both, ROWS, pairs)
    handed = jnp.where(zero, jnp.concatenate([bottom, far[h:]]), jnp.concatenate([top, far[:h]]))
    given = turn(handed, "core", 1)
    below = jnp.where(zero, jnp.concatenate([far[h:], far[:h]]), given)
    above = jnp.where(zero, given, far)
    return below, above


def turn(value, axis, by):
    size = lax.axis_size(axis)
    return lax.ppermute(value, axis, [(i, (i + by) % size) for i in range(size)])


def spread(value, axis):
    size = 1
    for name in axis if isinstance(axis, tuple) else (axis,):
        size *= lax.axis_size(name)
    copies = jnp.broadcast_to(value[None], (size,) + value.shape).reshape((size * value.shape[0],) + value.shape[1:])
    return lax.all_to_all(copies, axis, 0, 0, tiled=True)


def cross(left, right):
    return lax.dot_general(left, right, (((0,), (0,)), ((), ())), preferred_element_type=F32)


def rim(snaps, mass, coupling, rims, offset):
    h = snaps.shape[0]
    other = jnp.where(offset == 1, rims[:h], rims[h:]).astype(F32)
    terms = jnp.dot(coupling, other, precision=lax.Precision.HIGHEST, preferred_element_type=F32)
    return (mass[:, None] * snaps.astype(F32) + terms).astype(BF16)


def shards(snapshots, mass_diag, lower_coupling, upper_coupling, band_offsets, start_basis):
    block_rows, width = snapshots.shape
    h = lower_coupling.shape[1]
    total_rows = block_rows * lax.axis_size(ROWS)
    group = lax.axis_index("x")
    core = lax.axis_index("core")

    inner = (mass_diag[h : block_rows - h, None] * snapshots[h : block_rows - h].astype(F32)).astype(BF16)
    inner, top, bottom = lax.optimization_barrier((inner, snapshots[:h], snapshots[block_rows - h :]))
    below, above = neighbour_rims(top, bottom, core)
    rims = jnp.concatenate(
        [
            rim(top, mass_diag[:h], lower_coupling[0], below, band_offsets[0, 0]),
            rim(bottom, mass_diag[block_rows - h :], upper_coupling[0], above, band_offsets[0, 1]),
        ],
        axis=0,
    )

    late = (group >= GROUPS // 2).astype(jnp.int32)

    def halved(piece):
        part = piece.shape[0] // 2
        return lax.dynamic_slice_in_dim(piece, late * part, part, 0)

    own = [inner, rims]
    following = [turn(piece, "x", -1) for piece in own]
    behind = [turn(piece, "x", 1) for piece in own]
    blocks = [
        sum(cross(p, p) for p in own),
        sum(cross(f, p) for f, p in zip(following, own)),
        sum(cross(halved(f), halved(p)) for f, p in zip(following, behind)),
    ]
    partial = jnp.concatenate(blocks, axis=0)
    forward = jnp.concatenate(following, axis=0)
    partial, start = lax.optimization_barrier((partial, start_basis.T))
    lanes = width // 2
    keep = jnp.where(core == 0, partial[:, :lanes], partial[:, lanes:])
    give = jnp.where(core == 0, partial[:, lanes:], partial[:, :lanes])
    chip = keep + turn(give, "core", 1)
    across = turn(forward, "x", -1)
    sources = lax.axis_size(("y", "z"))
    pieces = lax.all_to_all(chip, ("y", "z"), 0, 0, tiled=True)
    share = pieces.reshape((sources, -1, lanes)).sum(0) / total_rows
    halves = spread(spread(share, "z"), ("x", "y"))
    other_halves = turn(halves, "core", 1)

    where = jnp.stack([group, core]).astype(jnp.int32)
    basis = iterate(where, halves, other_halves, start, ITERS)
    return modes(own, following, across, behind, basis, block_rows, h)


def solution(mesh):
    fine = jax.sharding.Mesh(mesh.devices.reshape(4, 8, 2, 4), ("y", "z", "core", "x"))
    placed = (
        P(ROWS, "x"),
        P(ROWS),
        P(ROWS, None, None),
        P(ROWS, None, None),
        P(ROWS, None),
        P(),
    )
    return jax.shard_map(shards, mesh=fine, in_specs=placed, out_specs=P(ROWS, "x"), check_vma=False)
```

```python
import functools

import jax
import jax.numpy as jnp
from jax import lax
from jax.experimental import pallas as pl
from jax.experimental.pallas import tpu as pltpu
from jax.sharding import PartitionSpec as P

F32 = jnp.float32
BF16 = jnp.bfloat16
GROUPS = 4
BLOCK = 128
TILE = 8
WINDOW = 16
ROW_COL = ((1,), (0,))
ROW_ROW = ((1,), (1,))


def split(value):
    high = value.astype(BF16)
    return high, (value - high.astype(F32)).astype(BF16)


def dot3(left, right, dims):
    one = lambda a, b: lax.dot_general(a, b, (dims, ((), ())), preferred_element_type=F32)
    return one(left[0], right[0]) + (one(left[0], right[1]) + one(left[1], right[0]))


def row(tile, index):
    return jnp.broadcast_to(tile[index : index + 1], tile.shape)


def column(tile, index):
    return jnp.broadcast_to(tile[:, index : index + 1], tile.shape)


def total(terms):
    while len(terms) > 1:
        terms = [sum(terms[i : i + 2][1:], terms[i]) for i in range(0, len(terms), 2)]
    return terms[0]


def inverse_block(m, beside):
    n = m.shape[0]
    tiles = WINDOW // TILE
    lanes = lax.broadcasted_iota(jnp.int32, (1, n), 1)
    subs = lax.broadcasted_iota(jnp.int32, (TILE, n), 0)
    done = []
    near = [m[s * TILE : (s + 1) * TILE] for s in range(tiles)]
    rest = m[WINDOW:]
    for k in range(0, n, WINDOW):
        for _ in range(-(-len(beside) * WINDOW // (n - k))):
            beside.pop(0)()
        inside = (lanes >= k) & (lanes < k + WINDOW)
        cols = [[column(near[s], k + j) for j in range((s + 1) * TILE)] for s in range(tiles)]
        rows = [
            jnp.where(inside, jnp.where(lanes == subs + (k + s * TILE), 1.0, 0.0), near[s]) for s in range(tiles)
        ]
        entry, pivot_row, inverse = {}, {}, {}
        for a in range(0, WINDOW, 2):
            b, t = a + 1, a // TILE
            for p in (a, b):
                entry[p] = {j: row(cols[j // TILE][p], j % TILE) for j in range(p, WINDOW)}
                pivot_row[p] = row(rows[t], p % TILE)
            aa, ab, bb = entry[a][a], entry[a][b], entry[b][b]
            inverse[a] = 1.0 / (aa * bb - ab * ab)
            for s in range(t, tiles):
                if s == t and b % TILE == TILE - 1:
                    continue
                to_a = cols[s][a] * bb - cols[s][b] * ab
                to_b = cols[s][b] * aa - cols[s][a] * ab
                if s == t:
                    later = subs > b % TILE
                    to_a, to_b = jnp.where(later, to_a, 0.0), jnp.where(later, to_b, 0.0)
                for j in range(b + 1, (s + 1) * TILE):
                    cols[s][j] = cols[s][j] - (to_a * entry[a][j] + to_b * entry[b][j]) * inverse[a]
                rows[s] = rows[s] - (to_a * pivot_row[a] + to_b * pivot_row[b]) * inverse[a]
        for s in range(tiles):
            out = None
            for a in range(s * TILE, (s + 1) * TILE, 2):
                b = a + 1
                aa, ab, bb = entry[a][a], entry[a][b], entry[b][b]
                scale = lax.rsqrt(aa)
                first = pivot_row[a] * scale
                second = (pivot_row[b] * aa - pivot_row[a] * ab) * (scale * lax.rsqrt(aa * bb - ab * ab))
                out = first if out is None else jnp.where(subs == a % TILE, first, out)
                out = jnp.where(subs == b % TILE, second, out)
            done.append(out)
        if k + WINDOW == n:
            break
        solved = [None] * WINDOW
        for a in reversed(range(0, WINDOW, 2)):
            b = a + 1
            aa, ab, bb = entry[a][a], entry[a][b], entry[b][b]
            va, vb = pivot_row[a], pivot_row[b]
            for j in reversed(range(b + 1, WINDOW)):
                va, vb = va - entry[a][j] * solved[j], vb - entry[b][j] * solved[j]
            solved[a] = (bb * va - ab * vb) * inverse[a]
            solved[b] = (aa * vb - ab * va) * inverse[a]
        near = []
        for s in range(tiles):
            x = rest[s * TILE : (s + 1) * TILE]
            near.append(jnp.where(inside, 0.0, x) - total([column(x, k + j) * solved[j] for j in range(WINDOW)]))
        if k + 2 * WINDOW < n:
            x = rest[WINDOW:]
            pieces = [jnp.zeros((k, n), F32)] if k else []
            for s in range(tiles):
                tile = solved[s * TILE]
                for a in range(1, TILE):
                    tile = jnp.where(subs == a, solved[s * TILE + a], tile)
                pieces.append(tile)
            pieces.append(jnp.zeros((n - k - WINDOW, n), F32))
            rest = jnp.where(inside, 0.0, x) - dot3(split(x), split(jnp.concatenate(pieces, axis=0)), ROW_COL)
    r = lax.broadcasted_iota(jnp.int32, (n, n), 0)
    c = lax.broadcasted_iota(jnp.int32, (n, n), 1)
    return jnp.where(r >= c, jnp.concatenate(done, axis=0), 0.0)


def inverse_factor(m_ref, beside):
    n = m_ref.shape[0]
    tasks = []
    d = m_ref[:BLOCK, :BLOCK]
    for j, lo in enumerate(range(0, n, BLOCK)):
        hi = lo + BLOCK
        w = inverse_block(d, tasks + beside(j))
        ws = split(w)
        tasks = [functools.partial(finish_row, m_ref, lo, hi, w, ws)]
        if hi == n:
            break
        end = hi + BLOCK
        near = split(dot3(split(m_ref[hi:end, lo:hi]), ws, ROW_ROW))
        d = m_ref[hi:end, hi:end] - dot3(near, near, ROW_ROW)
        tasks += [functools.partial(finish_rows, m_ref, lo, hi, hi, end, near, None, ws)]
        if end < n:
            tasks += [functools.partial(finish_rows, m_ref, lo, hi, end, n, None, near, ws)]
    for task in tasks:
        task()


def equilibrate(m_ref, scale_ref):
    n = m_ref.shape[0]
    eye = lax.broadcasted_iota(jnp.int32, (BLOCK, BLOCK), 0) == lax.broadcasted_iota(jnp.int32, (BLOCK, BLOCK), 1)
    across = []
    for lo in range(0, n, BLOCK):
        hi = lo + BLOCK
        diagonal = jnp.where(eye, m_ref[lo:hi, lo:hi], 0.0)
        across.append(lax.rsqrt(jnp.sum(diagonal, axis=0, keepdims=True)))
        down = lax.rsqrt(jnp.sum(diagonal, axis=1, keepdims=True))
        scale_ref[:, lo:hi] = jnp.broadcast_to(across[-1], (TILE, BLOCK))
        for j, factor in enumerate(across):
            part = slice(j * BLOCK, (j + 1) * BLOCK)
            m_ref[lo:hi, part] = m_ref[lo:hi, part] * (down * factor)


def finish_row(m_ref, lo, hi, w, ws):
    if lo:
        m_ref[lo:hi, :lo] = dot3(ws, split(m_ref[lo:hi, :lo]), ROW_COL)
    m_ref[lo:hi, lo:hi] = w


def finish_rows(m_ref, lo, hi, start, end, factor, near, ws):
    if factor is None:
        factor = split(dot3(split(m_ref[start:end, lo:hi]), ws, ROW_ROW))
        m_ref[start:end, hi:start] = m_ref[start:end, hi:start] - dot3(factor, near, ROW_ROW)
        m_ref[start:end, start:end] = m_ref[start:end, start:end] - dot3(factor, factor, ROW_ROW)
    m_ref[start:end, lo:hi] = -dot3(factor, ws, ROW_COL)
    if lo:
        m_ref[start:end, :lo] = m_ref[start:end, :lo] - dot3(factor, split(m_ref[lo:hi, :lo]), ROW_COL)


def assemble(core, mine_ref, other_ref, gh_ref, gl_ref):
    size = gh_ref.shape[0] // GROUPS
    part = size // 2
    halves = ((mine_ref, core * part), (other_ref, (1 - core) * part))

    def place(value, row_at, col_at):
        where = pl.ds(pl.multiple_of(row_at, part), value.shape[0]), pl.ds(pl.multiple_of(col_at, part), value.shape[1])
        gh_ref[where], gl_ref[where] = split(value)

    for group in range(GROUPS):
        own, after = group * size, ((group + 1) % GROUPS) * size
        lo = group * 3 * size
        for ref, at in halves:
            place(ref[lo : lo + size, :], own, own + at)
            value = ref[lo + size : lo + 2 * size, :]
            place(value, after, own + at)
            place(value.T, own + at, after)
    for group in range(GROUPS // 2):
        after, last = (group + 1) * size, ((group - 1) % GROUPS) * size
        lo, opposite = (group * 3 + 2) * size, ((group + 2) * 3 + 2) * size
        for ref, at in halves:
            for ref_across, at_across in halves:
                value = ref[pl.ds(pl.multiple_of(lo + at_across, part), part), :]
                value = value + ref_across[pl.ds(pl.multiple_of(opposite + at, part), part), :].T
                place(value, after + at_across, last + at)
                place(value.T, last + at, after + at_across)


def iterate_kernel(
    iters, where_ref, mine_ref, other_ref, start_ref, out_ref, gh_ref, gl_ref, image_ref, ih_ref, il_ref, next_ref, m_ref, scale_ref
):
    assemble(where_ref[1], mine_ref, other_ref, gh_ref, gl_ref)
    n = m_ref.shape[0]
    half = n // 2
    image_ref[...] = dot3(split(start_ref[...]), (gh_ref[...], gl_ref[...]), ROW_COL)

    def orthonormalise(i, carry):
        @pl.when(i > 0)
        def _():
            high, low = split(next_ref[...])
            for lo in (0, half):
                hi = lo + half
                weights = split(lower(m_ref, lo, hi) * scale_ref[:1, :hi])
                image_ref[lo:hi, :] = dot3(weights, (high[:hi], low[:hi]), ROW_COL)

        ih_ref[...], il_ref[...] = split(image_ref[...])
        for lo in (0, half):
            left = (ih_ref[lo : lo + half], il_ref[lo : lo + half])
            for to in range(0, lo + 1, half):
                right = (ih_ref[to : to + half], il_ref[to : to + half])
                m_ref[lo : lo + half, to : to + half] = dot3(left, right, ROW_ROW)

        def part_of_next(rows, cols):
            left = (ih_ref[rows, :], il_ref[rows, :])
            next_ref[rows, cols] = dot3(left, (gh_ref[:, cols], gl_ref[:, cols]), ROW_COL)

        def beside(j):
            rows = pl.ds(j * BLOCK, BLOCK)
            width = 2 * BLOCK
            return [functools.partial(part_of_next, rows, pl.ds(at, width)) for at in range(0, gh_ref.shape[1], width)]

        equilibrate(m_ref, scale_ref)
        inverse_factor(m_ref, beside)
        return carry

    lax.fori_loop(0, iters, orthonormalise, 0)
    cols = n // GROUPS
    at = pl.multiple_of(where_ref[0] * cols, cols)
    r = lax.broadcasted_iota(jnp.int32, (cols, n), 0) + at
    c = lax.broadcasted_iota(jnp.int32, (cols, n), 1)
    weights = split(jnp.where(r >= c, m_ref[pl.ds(at, cols), :], 0.0) * scale_ref[:1, :])
    basis = dot3(weights, (ih_ref[...], il_ref[...]), ROW_COL).astype(BF16)
    next_ref[:cols, :] = basis.astype(F32)
    size = out_ref.shape[1] // GROUPS
    for q in range(GROUPS):
        source = pl.multiple_of(lax.rem(where_ref[0] + q, GROUPS) * size, size)
        out_ref[:, q * size : (q + 1) * size] = next_ref[:cols, pl.ds(source, size)].astype(BF16)


def lower(m_ref, lo, hi):
    r = lax.broadcasted_iota(jnp.int32, (hi - lo, hi), 0) + lo
    c = lax.broadcasted_iota(jnp.int32, (hi - lo, hi), 1)
    return jnp.where(r >= c, m_ref[lo:hi, :hi], 0.0)


def iterate(where, mine, other, start, iters):
    k, n = start.shape
    return pl.pallas_call(
        functools.partial(iterate_kernel, iters),
        out_shape=jax.ShapeDtypeStruct((k // GROUPS, n), BF16),
        in_specs=[pl.BlockSpec(memory_space=pltpu.SMEM)] + [pl.BlockSpec(memory_space=pltpu.VMEM)] * 3,
        out_specs=pl.BlockSpec(memory_space=pltpu.VMEM),
        scratch_shapes=[
            pltpu.VMEM((n, n), BF16),
            pltpu.VMEM((n, n), BF16),
            pltpu.VMEM((k, n), F32),
            pltpu.VMEM((k, n), BF16),
            pltpu.VMEM((k, n), BF16),
            pltpu.VMEM((k, n), F32),
            pltpu.VMEM((k, k), F32),
            pltpu.VMEM((TILE, k), F32),
        ],
        compiler_params=pltpu.CompilerParams(vmem_limit_bytes=20 * 2**20),
        cost_estimate=pl.CostEstimate(flops=10**6, bytes_accessed=2**20, transcendentals=0),
    )(where, mine, other, start)


def modes_kernel(h, *refs):
    *whole, basis_ref, out_ref = refs
    across = whole.pop()
    inner, rims = whole[:3], whole[3:]
    rows = out_ref.shape[0]
    middle = rows - 2 * h
    size = basis_ref.shape[1] // GROUPS

    def project(refs, lo, hi, at):
        result = None
        for q, value in enumerate((refs[0][lo:hi, :], refs[1][lo:hi, :], across[at + lo : at + hi, :], refs[2][lo:hi, :])):
            part = basis_ref[:, q * size : (q + 1) * size]
            term = lax.dot_general(value, part, (ROW_ROW, ((), ())), preferred_element_type=F32)
            result = term if result is None else result + term
        return result

    out_ref[:h, :] = project(rims, 0, h, middle)
    out_ref[rows - h :, :] = project(rims, h, 2 * h, middle)
    out_ref[h : rows - h, :] = project(inner, 0, middle, 0)


def modes(own, following, across, behind, basis, rows, h):
    parts = [[p[i] for p in (own, following, behind)] for i in (0, 1)]
    return pl.pallas_call(
        functools.partial(modes_kernel, h),
        out_shape=jax.ShapeDtypeStruct((rows, basis.shape[0]), F32),
        in_specs=[pl.BlockSpec(memory_space=pltpu.VMEM)] * 8,
        out_specs=pl.BlockSpec(memory_space=pltpu.VMEM),
        compiler_params=pltpu.CompilerParams(vmem_limit_bytes=16 * 2**20),
    )(*parts[0], *parts[1], across, basis)


ITERS = 3
ROWS = ("y", "z", "core")


def neighbour_rims(top, bottom, core):
    blocks = lax.axis_size(ROWS)
    h = top.shape[0]
    zero = core == 0
    sibling = turn(jnp.where(zero, top, bottom), "core", 1)
    both = jnp.where(zero, jnp.concatenate([bottom, sibling]), jnp.concatenate([sibling, top]))
    pairs = [(i, i + 2 - 4 * (i % 2)) for i in range(blocks) if 0 <= i + 2 - 4 * (i % 2) < blocks]
    far = lax.ppermute(both, ROWS, pairs)
    handed = jnp.where(zero, jnp.concatenate([bottom, far[h:]]), jnp.concatenate([top, far[:h]]))
    given = turn(handed, "core", 1)
    below = jnp.where(zero, jnp.concatenate([far[h:], far[:h]]), given)
    above = jnp.where(zero, given, far)
    return below, above


def turn(value, axis, by):
    size = lax.axis_size(axis)
    return lax.ppermute(value, axis, [(i, (i + by) % size) for i in range(size)])


def spread(value, axis):
    size = 1
    for name in axis if isinstance(axis, tuple) else (axis,):
        size *= lax.axis_size(name)
    copies = jnp.broadcast_to(value[None], (size,) + value.shape).reshape((size * value.shape[0],) + value.shape[1:])
    return lax.all_to_all(copies, axis, 0, 0, tiled=True)


def cross(left, right):
    return lax.dot_general(left, right, (((0,), (0,)), ((), ())), preferred_element_type=F32)


def rim(snaps, mass, coupling, rims, offset):
    h = snaps.shape[0]
    other = jnp.where(offset == 1, rims[:h], rims[h:]).astype(F32)
    terms = jnp.dot(coupling, other, precision=lax.Precision.HIGHEST, preferred_element_type=F32)
    return (mass[:, None] * snaps.astype(F32) + terms).astype(BF16)


def shards(snapshots, mass_diag, lower_coupling, upper_coupling, band_offsets, start_basis):
    block_rows, width = snapshots.shape
    h = lower_coupling.shape[1]
    total_rows = block_rows * lax.axis_size(ROWS)
    group = lax.axis_index("x")
    core = lax.axis_index("core")

    inner = (mass_diag[h : block_rows - h, None] * snapshots[h : block_rows - h].astype(F32)).astype(BF16)
    inner, top, bottom = lax.optimization_barrier((inner, snapshots[:h], snapshots[block_rows - h :]))
    below, above = neighbour_rims(top, bottom, core)
    rims = jnp.concatenate(
        [
            rim(top, mass_diag[:h], lower_coupling[0], below, band_offsets[0, 0]),
            rim(bottom, mass_diag[block_rows - h :], upper_coupling[0], above, band_offsets[0, 1]),
        ],
        axis=0,
    )

    late = (group >= GROUPS // 2).astype(jnp.int32)

    def halved(piece):
        part = piece.shape[0] // 2
        return lax.dynamic_slice_in_dim(piece, late * part, part, 0)

    own = [inner, rims]
    following = [turn(piece, "x", -1) for piece in own]
    behind = [turn(piece, "x", 1) for piece in own]
    blocks = [
        sum(cross(p, p) for p in own),
        sum(cross(f, p) for f, p in zip(following, own)),
        sum(cross(halved(f), halved(p)) for f, p in zip(following, behind)),
    ]
    partial = jnp.concatenate(blocks, axis=0)
    forward = jnp.concatenate(following, axis=0)
    partial, start = lax.optimization_barrier((partial, start_basis.T))
    lanes = width // 2
    keep = jnp.where(core == 0, partial[:, :lanes], partial[:, lanes:])
    give = jnp.where(core == 0, partial[:, lanes:], partial[:, :lanes])
    chip = keep + turn(give, "core", 1)
    across = turn(forward, "x", -1)
    sources = lax.axis_size(("y", "z"))
    pieces = lax.all_to_all(chip, ("y", "z"), 0, 0, tiled=True)
    share = pieces.reshape((sources, -1, lanes)).sum(0) / total_rows
    halves = spread(spread(share, "z"), ("x", "y"))
    other_halves = turn(halves, "core", 1)

    where = jnp.stack([group, core]).astype(jnp.int32)
    basis = iterate(where, halves, other_halves, start, ITERS)
    return modes(own, following, across, behind, basis, block_rows, h)


def solution(mesh):
    fine = jax.sharding.Mesh(mesh.devices.reshape(4, 8, 2, 4), ("y", "z", "core", "x"))
    placed = (
        P(ROWS, "x"),
        P(ROWS),
        P(ROWS, None, None),
        P(ROWS, None, None),
        P(ROWS, None),
        P(),
    )
    return jax.shard_map(shards, mesh=fine, in_specs=placed, out_specs=P(ROWS, "x"), check_vma=False)
```
